512 devices in a mesh: outer: 16 (over y, core), inner: 8 (over z), region: 4 (over x).
Axes of the slice: x: 4, y: 8, z: 8, core: 2. Of those that a mesh axis runs over, the one named last changes fastest.
Arguments:
- observations: float32 [1024, 128], P(('region', 'outer', 'inner')), parts along dimension 0, may hold values from -6 to 6
- obs_mask: int32 [1024, 128], P(('region', 'outer', 'inner')), parts along dimension 0, may hold values 0 or 1
- sensor_map: int32 [512], P('region'), parts along dimension 0, may hold values from 0 to 127
- transition: float32 [128, 128], replicated, may hold values from -1 to 1
- proc_noise: float32 [128, 128], replicated, may hold values from -1 to 1, as said below
- obs_var: float32 [128], replicated, may hold values from 0.1 to 1
- prior_mean: float32 [512], P('region'), parts along dimension 0, may hold values from -6 to 6
- prior_var: float32 [512], P('region'), parts along dimension 0, may hold values from 0.5 to 4
Outputs:
- filt_mean: float32 [1024, 128], P(('region', 'outer', 'inner')), parts along dimension 0
- filt_cov: float32 [1024, 128, 128], P(('region', 'outer', 'inner')), parts along dimension 0
The draws below stay inside these ranges and needn't reach their ends.
There are 4 independent parts, one for each index of `region`. The reference program is written for one: setup_inputs(seed, part) draws one part's arguments, and reference() takes and returns one part's arrays. A program takes and returns all parts, laid end to end along the dimension named above; an argument that names none is the same for every part. Nothing has to cross between parts.
Inputs may be any that keep to these rules, and one draw needn't show every extreme that they name: `proc_noise`: symmetric positive definite.
All inputs are finite; a program needn't handle non-finite values. No bound on the sum of `obs_mask` on one device may be relied on, other than what follows from the above.
Results may differ from the reference program's by a relative error of at most 0.00017.
Values sent between devices are 32-bit elements; how exact they have to be, the bound alone decides.
A program may use at most 128 MiB of HBM per device.

```python
import math
import jax
import jax.numpy as jnp
from jax import lax

S = 128
M = 128
TIME = 256


def draw_transition(key, part):
    rate_key, couple_key = jax.random.split(jax.random.fold_in(key, 11))
    rates = jnp.exp(jax.random.uniform(rate_key, (S,), jnp.float32, math.log(0.3 / TIME), math.log(1.0 / 30.0)))
    couple = jax.random.truncated_normal(couple_key, -3.0, 3.0, (S, S), jnp.float32)
    ident_mat = jnp.eye(S, dtype=jnp.float32)
    return jnp.diag(jnp.exp(-rates)) + couple * (1.0 - ident_mat) * (0.1 / math.sqrt(S))


def draw_proc_noise(key, part):
    level_key, couple_key = jax.random.split(jax.random.fold_in(key, 23))
    levels = jnp.exp(jax.random.uniform(level_key, (S,), jnp.float32, math.log(0.05), math.log(0.5)))
    couple = jax.random.uniform(couple_key, (S, S), jnp.float32, -1.0, 1.0)
    ident_mat = jnp.eye(S, dtype=jnp.float32)
    paired = 0.5 * (couple + couple.T) * (1.0 - ident_mat) * (0.9 * 0.05 / S)
    return jnp.diag(levels) + paired


def place_ends(drawn, key, low, largest):
    longest = drawn.shape.index(max(drawn.shape))
    spots = []
    for shift in (0, 1):
        where = [jax.random.randint(jax.random.fold_in(key, axis), (), 0, length) for axis, length in enumerate(drawn.shape)]
        where[longest] = (where[longest] + shift) % drawn.shape[longest]
        spots.append(tuple(where))
    return drawn.at[spots[0]].set(low).at[spots[1]].set(largest)


def shard_levels(own_key, dims, pieces, low, high):
    def one(position, blocks):
        draws = jax.random.uniform(jax.random.fold_in(jax.random.fold_in(own_key, 6), position), (blocks,), jnp.float32, low / len(pieces), high / len(pieces))
        return jnp.repeat(jnp.exp(draws), dims[position] // blocks).reshape((-1,) + (1,) * (len(dims) - position - 1))

    factor_of = one(*pieces[0])
    for cut in pieces[1:]:
        factor_of = factor_of * one(*cut)
    return factor_of


def gaussian(key, extent, deviation, bound, pieces=(), held_as=jnp.bfloat16):
    result = jax.random.normal(key, extent, jnp.float32) * deviation
    if len(pieces) > 0:
        result = shard_levels(key, extent, pieces, -0.22, 0.18) * result
    return jnp.clip(result, min=-bound, max=bound).astype(held_as)


def setup_inputs(seed: int = 0, part: int = 0) -> dict:
    splits = jax.random.split(jax.random.key(seed), 9)
    part_keys = jax.random.split(jax.random.fold_in(splits[8], part), 9)
    return {
        "observations": gaussian(part_keys[0], (TIME, M), 1.0, 6.0, ((0, 128),), jnp.float32),
        "obs_mask": place_ends((jax.random.randint(part_keys[1], (TIME, M), 0, 4) < 3).astype(jnp.int32), jax.random.fold_in(part_keys[1], 1), 0, 1),
        "sensor_map": place_ends(jax.random.randint(part_keys[2], (M,), 0, S), jax.random.fold_in(part_keys[2], 1), 0, S - 1).astype(jnp.int32),
        "transition": draw_transition(jax.random.fold_in(splits[8], 71), part),
        "proc_noise": draw_proc_noise(jax.random.fold_in(splits[8], 71), part),
        "obs_var": jnp.clip(jnp.exp(jax.random.uniform(splits[5], (M,), jnp.float32, math.log(0.1), math.log(1.0))), 0.1, 1.0),
        "prior_mean": gaussian(part_keys[6], (S,), 1.0, 6.0, (), jnp.float32),
        "prior_var": jnp.clip(jnp.exp(jax.random.uniform(part_keys[7], (S,), jnp.float32, math.log(0.5), math.log(4.0))), 0.5, 4.0),
    }


def highest(left, right):
    return jnp.dot(left, right, precision=lax.Precision.HIGHEST)

def filter_step(carried, inputs, transition, proc_noise, sensor_map, obs_var):
    prev_mean, prev_cov = carried
    observed, mask_row = inputs
    weights = mask_row.astype(jnp.float32)
    pred_mean = highest(transition, prev_mean)
    pred_cov = highest(highest(transition, prev_cov), transition.T) + proc_noise
    picked = pred_cov[sensor_map] * weights[:, None]
    innov_cov = picked[:, sensor_map] * weights[None, :] + jnp.diag(obs_var)
    factor = jnp.linalg.cholesky(innov_cov)
    solved = jax.scipy.linalg.cho_solve((factor, True), picked)
    innovation = weights * (observed - pred_mean[sensor_map])
    new_mean = pred_mean + highest(solved.T, innovation)
    new_cov = pred_cov - highest(picked.T, solved)
    new_cov = 0.5 * (new_cov + new_cov.T)
    return ((new_mean, new_cov), (new_mean, new_cov))

def reference(observations, obs_mask, sensor_map, transition, proc_noise, obs_var, prior_mean, prior_var):
    start_state = (prior_mean, jnp.diag(prior_var))

    def advance(carried, inputs):
        return filter_step(carried, inputs, transition, proc_noise, sensor_map, obs_var)
    last_state, outputs = lax.scan(advance, start_state, (observations, obs_mask))
    return (outputs[0], outputs[1])
```

```python
import functools

import jax
import jax.numpy as jnp
from jax import lax
from jax.experimental import pallas as pl
from jax.experimental.pallas import tpu as pltpu
from jax.sharding import PartitionSpec as P

N = 128
BF = jnp.bfloat16
F32 = jnp.float32
BLOCK = 32
NN = (((1,), (0,)), ((), ()))
NT = (((1,), (1,)), ((), ()))
TN = (((0,), (0,)), ((), ()))
MESH = pl.DeviceIdType.MESH


def dot(left, right, dims):
    return lax.dot_general(
        left, right, dims, precision=lax.Precision.HIGHEST, preferred_element_type=F32
    )


def iota(dim, shape=(N, N)):
    return lax.broadcasted_iota(jnp.int32, shape, dim)


def split3(x):
    high = x.astype(BF)
    rest = x - high.astype(F32)
    mid = rest.astype(BF)
    return high, mid, (rest - mid.astype(F32)).astype(BF)


def factor(S, tiles, floors=None, done=None):
    sub, lane = iota(0, (8, N)), iota(1, (8, N))
    groups = BLOCK // 8
    for row0 in range(0, N, BLOCK):
        panel = [
            [S[row0 + 8 * q : row0 + 8 * q + 8, N * c : N * c + N] for q in range(groups)]
            for c in range(tiles)
        ]
        cols = [
            [
                jnp.broadcast_to(panel[0][q][:, row0 + k : row0 + k + 1], (8, N))
                if q >= k // 8
                else None
                for q in range(groups)
            ]
            for k in range(BLOCK)
        ]
        scale = [jnp.zeros((8, N), F32) for _ in range(groups)]
        raised = [jnp.zeros((8, N), F32) for _ in range(groups)]
        for j in range(BLOCK):
            r, s = j // 8, j % 8
            pivot = jnp.broadcast_to(cols[j][r][s : s + 1, :], (8, N))
            if floors is not None:
                low = jnp.broadcast_to(floors[row0 // 8 + r][s : s + 1, :], (8, N))
                kept = jnp.maximum(pivot, low)
                raised[r] = jnp.where(sub == s, kept - pivot, raised[r])
                pivot = kept
            inverse, root = 1.0 / pivot, lax.rsqrt(pivot)
            scale[r] = jnp.where(sub == s, root, scale[r])
            mult = [cols[j][q] * inverse if q >= r else None for q in range(groups)]
            if s < 7:
                below = jnp.where(sub > s, mult[r], 0.0)
            for c in range(tiles):
                line = jnp.broadcast_to(panel[c][r][s : s + 1, :], (8, N))
                if s < 7:
                    panel[c][r] = panel[c][r] - below * line
                for q in range(r + 1, groups):
                    panel[c][q] = panel[c][q] - mult[q] * line
            for k in range(j + 1, BLOCK):
                line = jnp.broadcast_to(cols[j][k // 8][k % 8 : k % 8 + 1, :], (8, N))
                for q in range(k // 8, groups):
                    cols[k][q] = cols[k][q] - mult[q] * line
        for q in range(groups):
            if floors is not None:
                diagonal = lane == sub + (row0 + 8 * q)
                panel[0][q] = panel[0][q] + jnp.where(diagonal, raised[q], 0.0)
            for c in range(tiles):
                panel[c][q] = panel[c][q] * scale[q]
                S[row0 + 8 * q : row0 + 8 * q + 8, N * c : N * c + N] = panel[c][q]
        if done is not None:
            done(row0, panel[0])
        if row0 + BLOCK < N:
            row1 = row0 + BLOCK
            whole = jnp.concatenate(
                [jnp.concatenate([panel[c][q] for c in range(tiles)], axis=1) for q in range(groups)],
                axis=0,
            )
            h, m, l = split3(whole)
            right = jnp.concatenate([h, m, h, l, h, m], axis=0)
            h, m, l = h[:, :N], m[:, :N], l[:, :N]
            left = jnp.concatenate([h, h, m, h, l, m], axis=0)
            update = lax.dot_general(left, right, TN, preferred_element_type=F32)
            S[row1:, :] = S[row1:, :] - update[row1:, :]


def cholesky(S, C, out, sent=None):
    eye = iota(0) == iota(1)
    S[...] = C
    low = jnp.sum(jnp.where(eye, C, 0.0), axis=1, keepdims=True) * 2e-7 + 1e-30
    low = jnp.broadcast_to(low, (N, N))
    sub, lane = iota(0, (8, N)), iota(1, (8, N))

    def done(row0, lines):
        for q in range(BLOCK // 8):
            row = row0 + 8 * q
            out[row : row + 8, :] = jnp.where(lane >= sub + row, lines[q], 0.0)
        if sent is not None:
            sent(row0 // BLOCK)

    factor(S, 1, [low[8 * q : 8 * q + 8, :] for q in range(N // 8)], done)


def kernel(
    outer, inner,
    obs_ref, mask_ref, map_ref, F_ref, Q_ref, r_ref, pm_ref, pv_ref,
    mean_ref, cov_ref,
    oU, ob, oAJ, rU, rb, rAJ, C, S, SC, gzs, gzr,
    send_sem, recv_sem, gz_sem,
):
    devices = outer * inner
    levels = devices.bit_length() - 1
    me_o, me_i, me_r = lax.axis_index("outer"), lax.axis_index("inner"), lax.axis_index("region")
    d = me_o * inner + me_i

    def place(index):
        return (index // inner, index % inner, me_r)

    barrier = pltpu.get_barrier_semaphore()
    targets = jnp.int32(0)
    for k in range(levels):
        @pl.when(d >= 2**k)
        def _():
            pl.semaphore_signal(barrier, inc=1, device_id=place(d - 2**k), device_id_type=MESH)
        targets = targets + jnp.where(d + 2**k < devices, 1, 0)

    one_hot = jnp.where(iota(0) == jnp.broadcast_to(map_ref[...], (N, N)), 1.0, 0.0)
    weight = mask_ref[...].astype(F32) / r_ref[...]
    rows = jnp.concatenate([weight, weight * obs_ref[...], jnp.zeros((4, N), F32)], axis=0)
    gzs[...] = dot(rows, one_hot, NT)

    @pl.when(targets > 0)
    def _():
        pl.semaphore_wait(barrier, targets)

    def gz_copy(to):
        return pltpu.make_async_remote_copy(
            src_ref=gzs, dst_ref=gzr, send_sem=gz_sem.at[0], recv_sem=gz_sem.at[1],
            device_id=place(to), device_id_type=MESH,
        )

    @pl.when(d + 1 < devices)
    def _():
        gz_copy(d + 1).start()

    eye = iota(0) == iota(1)
    zero8 = jnp.zeros((8, N), F32)
    row8 = iota(0, (8, N))
    C[...] = Q_ref[...]
    ob[0] = zero8
    oAJ[0, 0:N, :] = F_ref[...]
    S[...] = jnp.zeros_like(S)
    prior = jnp.where(eye, jnp.broadcast_to(pv_ref[...], (N, N)), 0.0)
    cholesky(SC, jnp.where(d == 0, prior, Q_ref[...]), rU.at[0])

    @pl.when(d == 0)
    def _():
        oAJ[0, N:, :] = jnp.zeros((N + 8, N), F32)
        rb[0] = jnp.where(row8 == 0, jnp.broadcast_to(pm_ref[...], (8, N)), 0.0)

    @pl.when(d > 0)
    def _():
        gz_copy(d).wait_recv()
        for ref, step in ((rAJ, 0), (oAJ, 1)):
            g, z = gzr[step : step + 1, :], gzr[2 + step : 3 + step, :]
            ref[0, N : 2 * N, :] = jnp.where(eye, jnp.broadcast_to(g, (N, N)), 0.0)
            ref[0, 2 * N :, :] = jnp.where(row8 == 0, jnp.broadcast_to(z, (8, N)), 0.0)
        rAJ[0, 0:N, :] = F_ref[...]
        rb[0] = zero8

    def remote(source, target, slot, which, to):
        return pltpu.make_async_remote_copy(
            src_ref=source, dst_ref=target,
            send_sem=send_sem.at[slot, which], recv_sem=recv_sem.at[slot, which],
            device_id=place(to), device_id_type=MESH,
        )

    blocks = N // BLOCK

    def copy_U(slot, p, to):
        lines = pl.ds(p * BLOCK, BLOCK)
        return remote(oU.at[slot, lines], rU.at[slot, lines], slot, p, to)

    def copy_b(slot, to):
        return remote(ob.at[slot], rb.at[slot], slot, blocks, to)

    def copy_AJ(slot, to):
        return remote(oAJ.at[slot], rAJ.at[slot], slot, blocks + 1, to)

    def level(i, ahead):
        back = ahead // 2
        full = d >= ahead
        goes = d + ahead < devices

        @pl.when(d >= back)
        def _():
            @pl.when(i > 0)
            def _():
                copy_b(i, d).wait_recv()
                for p in range(blocks):
                    copy_U(i, p, d).wait_recv()

            U, b1, A2, eta2 = rU[i], rb[i], oAJ[i, 0:N, :], oAJ[i, 2 * N :, :]
            UJ = dot(U, oAJ[i, N : 2 * N, :], NT)
            S[:, 0:N] = dot(UJ, U, NT) + jnp.where(eye, 1.0, 0.0)
            S[:, N : 2 * N] = dot(U, A2, NT)
            S[:, 2 * N : 3 * N] = UJ
            S[:, 3 * N : 3 * N + 8] = dot(U, eta2, NT) - dot(UJ, b1, NT)
            factor(S, 4)
            KY = S[:, N : 2 * N]
            gram = dot(jnp.concatenate([KY, S[:, 3 * N :]], axis=1), KY, TN)
            new_C = C[...] + gram[0:N, :]
            C[...] = new_C
            ob[i + 1] = ob[i] + dot(b1, A2, NT) + gram[N : N + 8, :]

            @pl.when(goes)
            def _():
                copy_b(i + 1, d + ahead).start()
                cholesky(SC, new_C, oU.at[i + 1], lambda p: copy_U(i + 1, p, d + ahead).start())

        @pl.when(d < back)
        def _():
            oU[i + 1] = oU[i]
            ob[i + 1] = ob[i]

            @pl.when(goes)
            def _():
                copy_b(i + 1, d + ahead).start()
                for p in range(blocks):
                    copy_U(i + 1, p, d + ahead).start()

        @pl.when(full)
        def _():
            @pl.when(i > 0)
            def _():
                copy_AJ(i, d).wait_recv()

            A1, J2 = rAJ[i, 0:N, :], oAJ[i, N : 2 * N, :]
            q = oAJ[i, 2 * N :, :] - dot(rb[i], J2, NT)
            KR = dot(S[:, 2 * N : 3 * N], A1, NN)
            others = dot(jnp.concatenate([oAJ[i, 0 : 2 * N, :], q], axis=0), A1, NN)
            gram = dot(jnp.concatenate([KR, S[:, N : 2 * N], S[:, 3 * N :]], axis=1), KR, TN)
            moved = dot(A1, others[N : 2 * N, :], TN)
            oAJ[i + 1, 0:N, :] = others[0:N, :] - gram[N : 2 * N, :]
            oAJ[i + 1, N : 2 * N, :] = rAJ[i, N : 2 * N, :] + moved - gram[0:N, :]
            oAJ[i + 1, 2 * N :, :] = (
                rAJ[i, 2 * N :, :] + others[2 * N :, :] - gram[2 * N : 2 * N + 8, :]
            )

            @pl.when(goes)
            def _():
                copy_AJ(i + 1, d + ahead).start()

        return ahead * 2

    lax.fori_loop(0, levels + 1, level, jnp.int32(1))

    cov = C[...]
    mean = ob[levels + 1]
    for step in range(2):
        g, z = gzs[step : step + 1, :], gzs[2 + step : 3 + step, :]
        across = jnp.broadcast_to(jnp.sqrt(g), (N, N))
        down = across.T
        scaled = down * cov
        S[:, 0:N] = scaled * across + jnp.where(eye, 1.0, 0.0)
        S[:, N : 2 * N] = scaled
        if step == 0:
            cov_F = dot(cov, F_ref[...], NT)
            S[:, 2 * N : 3 * N] = down * cov_F
            spread = dot(F_ref[...], cov_F, NN)
            tiles = 3
        else:
            tiles = 2
        factor(S.at[:, 0 : tiles * N], tiles)
        K = S[:, N : 2 * N]
        new_cov = cov - dot(K, K, TN)
        new_cov = 0.5 * (new_cov + new_cov.T)
        cov_ref[step] = new_cov
        new_mean = mean + dot(z - g * mean, new_cov, NN)
        mean_ref[step : step + 1, :] = new_mean[0:1, :]
        if step == 0:
            K = S[:, 2 * N : 3 * N]
            cov = spread + Q_ref[...] - dot(K, K, TN)
            cov = 0.5 * (cov + cov.T)
            mean = dot(new_mean, F_ref[...], NT)

    @pl.when(d + 1 < devices)
    def _():
        gz_copy(d + 1).wait_send()

    def drain(i, ahead):
        @pl.when(d + ahead < devices)
        def _():
            copy_b(i + 1, d + ahead).wait_send()
            for p in range(blocks):
                copy_U(i + 1, p, d + ahead).wait_send()

            @pl.when(d >= ahead)
            def _():
                copy_AJ(i + 1, d + ahead).wait_send()

        return ahead * 2

    lax.fori_loop(0, levels, drain, jnp.int32(1))


def local(outer, inner, obs, mask, smap, F, Q, r, pm, pv):
    devices = outer * inner
    levels = devices.bit_length() - 1
    vmem = pl.BlockSpec(memory_space=pltpu.VMEM)
    slots = levels + 2
    return pl.pallas_call(
        functools.partial(kernel, outer, inner),
        out_shape=(
            jax.ShapeDtypeStruct((2, N), F32),
            jax.ShapeDtypeStruct((2, N, N), F32),
        ),
        in_specs=[vmem] * 8,
        out_specs=(vmem, vmem),
        scratch_shapes=[
            pltpu.VMEM((slots, N, N), F32),
            pltpu.VMEM((slots, 8, N), F32),
            pltpu.VMEM((slots, 2 * N + 8, N), F32),
            pltpu.VMEM((slots, N, N), F32),
            pltpu.VMEM((slots, 8, N), F32),
            pltpu.VMEM((slots, 2 * N + 8, N), F32),
            pltpu.VMEM((N, N), F32),
            pltpu.VMEM((N, 4 * N), F32),
            pltpu.VMEM((N, N), F32),
            pltpu.VMEM((8, N), F32),
            pltpu.VMEM((8, N), F32),
            pltpu.SemaphoreType.DMA((slots, N // BLOCK + 2)),
            pltpu.SemaphoreType.DMA((slots, N // BLOCK + 2)),
            pltpu.SemaphoreType.DMA((2,)),
        ],
        compiler_params=pltpu.CompilerParams(
            collective_id=0, has_side_effects=True, vmem_limit_bytes=48 * 1024 * 1024
        ),
    )(obs, mask, smap.reshape(1, N), F, Q, r.reshape(1, N), pm.reshape(1, N), pv.reshape(1, N))


def solution(mesh):
    outer, inner = mesh.shape["outer"], mesh.shape["inner"]
    split = P(("region", "outer", "inner"))
    return jax.shard_map(
        functools.partial(local, outer, inner),
        mesh=mesh,
        in_specs=(split, split, P("region"), P(), P(), P(), P("region"), P("region")),
        out_specs=(split, split),
        check_vma=False,
    )
```

```python
import functools

import jax
import jax.numpy as jnp
from jax import lax
from jax.experimental import pallas as pl
from jax.experimental.pallas import tpu as pltpu
from jax.sharding import PartitionSpec as P

N = 128
BF = jnp.bfloat16
F32 = jnp.float32
BLOCK = 32
NN = (((1,), (0,)), ((), ()))
NT = (((1,), (1,)), ((), ()))
TN = (((0,), (0,)), ((), ()))
MESH = pl.DeviceIdType.MESH


def dot(left, right, dims):
    return lax.dot_general(
        left, right, dims, precision=lax.Precision.HIGHEST, preferred_element_type=F32
    )


def iota(dim, shape=(N, N)):
    return lax.broadcasted_iota(jnp.int32, shape, dim)


def split3(x):
    high = x.astype(BF)
    rest = x - high.astype(F32)
    mid = rest.astype(BF)
    return high, mid, (rest - mid.astype(F32)).astype(BF)


def factor(*jobs):
    sub = iota(0, (8, N))
    groups = BLOCK // 8
    for row0 in range(0, N, BLOCK):
        work = []
        for S, tiles in jobs:
            panel = [
                [S[row0 + 8 * q : row0 + 8 * q + 8, N * c : N * c + N] for q in range(groups)]
                for c in range(tiles)
            ]
            cols = [
                [
                    jnp.broadcast_to(panel[0][q][:, row0 + k : row0 + k + 1], (8, N))
                    if q >= k // 8
                    else None
                    for q in range(groups)
                ]
                for k in range(BLOCK)
            ]
            scale = [jnp.zeros((8, N), F32) for _ in range(groups)]
            work.append((S, tiles, panel, cols, scale))
        for j in range(BLOCK):
            r, s = j // 8, j % 8
            for S, tiles, panel, cols, scale in work:
                pivot = jnp.broadcast_to(cols[j][r][s : s + 1, :], (8, N))
                inverse = 1.0 / pivot
                scale[r] = jnp.where(sub == s, lax.rsqrt(pivot), scale[r])
                mult = [cols[j][q] * inverse if q >= r else None for q in range(groups)]
                if s < 7:
                    below = jnp.where(sub > s, mult[r], 0.0)
                for k in range(j + 1, BLOCK):
                    line = jnp.broadcast_to(cols[j][k // 8][k % 8 : k % 8 + 1, :], (8, N))
                    for q in range(k // 8, groups):
                        cols[k][q] = cols[k][q] - mult[q] * line
                for c in range(tiles):
                    line = jnp.broadcast_to(panel[c][r][s : s + 1, :], (8, N))
                    if s < 7:
                        panel[c][r] = panel[c][r] - below * line
                    for q in range(r + 1, groups):
                        panel[c][q] = panel[c][q] - mult[q] * line
        for S, tiles, panel, cols, scale in work:
            for q in range(groups):
                for c in range(tiles):
                    panel[c][q] = panel[c][q] * scale[q]
                    S[row0 + 8 * q : row0 + 8 * q + 8, N * c : N * c + N] = panel[c][q]
        if row0 + BLOCK < N:
            row1 = row0 + BLOCK
            for S, tiles, panel, cols, scale in work:
                whole = jnp.concatenate(
                    [
                        jnp.concatenate([panel[c][q] for c in range(tiles)], axis=1)
                        for q in range(groups)
                    ],
                    axis=0,
                )
                h, m, l = split3(whole)
                right = jnp.concatenate([h, m, h, l, h, m], axis=0)
                h, m, l = h[:, :N], m[:, :N], l[:, :N]
                left = jnp.concatenate([h, h, m, h, l, m], axis=0)
                update = lax.dot_general(left, right, TN, preferred_element_type=F32)
                S[row1:, :] = S[row1:, :] - update[row1:, :]


def kernel(
    outer, inner,
    obs_ref, mask_ref, map_ref, F_ref, Q_ref, r_ref, pm_ref, pv_ref,
    mean_ref, cov_ref,
    oL, ob, oAJ, rL, rb, rAJ, B, M, S, T, gzs, gzr,
    send_sem, recv_sem, gz_sem,
):
    devices = outer * inner
    levels = devices.bit_length() - 1
    me_o, me_i, me_r = lax.axis_index("outer"), lax.axis_index("inner"), lax.axis_index("region")
    d = me_o * inner + me_i

    def place(index):
        return (index // inner, index % inner, me_r)

    barrier = pltpu.get_barrier_semaphore()
    targets = jnp.int32(0)
    for k in range(levels):
        @pl.when(d >= 2**k)
        def _():
            pl.semaphore_signal(barrier, inc=1, device_id=place(d - 2**k), device_id_type=MESH)
        targets = targets + jnp.where(d + 2**k < devices, 1, 0)

    one_hot = jnp.where(iota(0) == jnp.broadcast_to(map_ref[...], (N, N)), 1.0, 0.0)
    weight = mask_ref[...].astype(F32) / r_ref[...]
    rows = jnp.concatenate([weight, weight * obs_ref[...], jnp.zeros((4, N), F32)], axis=0)
    gzs[...] = dot(rows, one_hot, NT)

    @pl.when(targets > 0)
    def _():
        pl.semaphore_wait(barrier, targets)

    def gz_copy(to):
        return pltpu.make_async_remote_copy(
            src_ref=gzs, dst_ref=gzr, send_sem=gz_sem.at[0], recv_sem=gz_sem.at[1],
            device_id=place(to), device_id_type=MESH,
        )

    @pl.when(d + 1 < devices)
    def _():
        gz_copy(d + 1).start()

    eye = iota(0) == iota(1)
    zero8 = jnp.zeros((8, N), F32)
    row8 = iota(0, (8, N))
    ob[0] = zero8
    S[...] = jnp.zeros_like(S)
    unit = jnp.where(eye, 1.0, 0.0)
    F = F_ref[...]
    T[:, 0:N] = Q_ref[...]
    T[:, N:] = unit
    factor((T, 2))
    K = T[:, N:]
    inverse = dot(K, K, TN)
    oL[0] = inverse
    oAJ[0, 0:N, :] = F
    FL = dot(F, inverse, TN)
    B[...] = FL
    M[...] = dot(FL, F, NN)

    @pl.when(d == 0)
    def _():
        oAJ[0, N:, :] = jnp.zeros((N + 8, N), F32)
        rL[0] = jnp.where(eye, 1.0 / jnp.broadcast_to(pv_ref[...], (N, N)), 0.0)
        rb[0] = jnp.where(row8 == 0, jnp.broadcast_to(pm_ref[...], (8, N)), 0.0)

    @pl.when(d > 0)
    def _():
        gz_copy(d).wait_recv()
        for ref, step in ((rAJ, 0), (oAJ, 1)):
            g, z = gzr[step : step + 1, :], gzr[2 + step : 3 + step, :]
            ref[0, N : 2 * N, :] = jnp.where(eye, jnp.broadcast_to(g, (N, N)), 0.0)
            ref[0, 2 * N :, :] = jnp.where(row8 == 0, jnp.broadcast_to(z, (8, N)), 0.0)
        rAJ[0, 0:N, :] = F
        rL[0] = inverse
        rb[0] = zero8

    def remote(source, target, slot, which, to):
        return pltpu.make_async_remote_copy(
            src_ref=source, dst_ref=target,
            send_sem=send_sem.at[slot, which], recv_sem=recv_sem.at[slot, which],
            device_id=place(to), device_id_type=MESH,
        )

    def copy_L(slot, to):
        return remote(oL.at[slot], rL.at[slot], slot, 0, to)

    def copy_b(slot, to):
        return remote(ob.at[slot], rb.at[slot], slot, 1, to)

    def copy_AJ(slot, to):
        return remote(oAJ.at[slot], rAJ.at[slot], slot, 2, to)

    def level(i, ahead):
        back = ahead // 2
        full = d >= ahead
        goes = d + ahead < devices

        @pl.when(d >= back)
        def _():
            J2, A2 = oAJ[i, N : 2 * N, :], oAJ[i, 0:N, :]
            S[:, N : 2 * N] = J2
            S[:, 2 * N : 3 * N] = A2.T
            T[:, N:] = B[...]

            @pl.when(i > 0)
            def _():
                copy_b(i, d).wait_recv()
                copy_L(i, d).wait_recv()

            b1 = rb[i]
            middle = rL[i] + J2
            S[:, 0:N] = middle
            T[:, 0:N] = middle + M[...]
            q = oAJ[i, 2 * N :, :] - dot(b1, J2, NT)
            S[:, 3 * N : 3 * N + 8] = q.T
            factor((T, 2), (S, 4))
            KB = T[:, N:]
            oL[i + 1] = oL[i] - dot(KB, KB, TN)

            @pl.when(goes)
            def _():
                copy_L(i + 1, d + ahead).start()

            ob[i + 1] = ob[i] + dot(b1, A2, NT) + dot(S[:, 3 * N : 3 * N + 8], S[:, 2 * N : 3 * N], TN)

        @pl.when(d < back)
        def _():
            oL[i + 1] = oL[i]
            ob[i + 1] = ob[i]

            @pl.when(goes)
            def _():
                copy_L(i + 1, d + ahead).start()

        @pl.when(goes)
        def _():
            copy_b(i + 1, d + ahead).start()

        @pl.when(full)
        def _():
            @pl.when(i > 0)
            def _():
                copy_AJ(i, d).wait_recv()

            A1, J2 = rAJ[i, 0:N, :], oAJ[i, N : 2 * N, :]
            q = oAJ[i, 2 * N :, :] - dot(rb[i], J2, NT)
            KR = dot(S[:, N : 2 * N], A1, NN)
            others = dot(jnp.concatenate([oAJ[i, 0 : 2 * N, :], q], axis=0), A1, NN)
            gram = dot(jnp.concatenate([KR, S[:, 2 * N :]], axis=1), KR, TN)
            moved = dot(A1, others[N : 2 * N, :], TN)
            A = others[0:N, :] - gram[N : 2 * N, :]
            oAJ[i + 1, 0:N, :] = A
            oAJ[i + 1, N : 2 * N, :] = rAJ[i, N : 2 * N, :] + moved - gram[0:N, :]
            oAJ[i + 1, 2 * N :, :] = (
                rAJ[i, 2 * N :, :] + others[2 * N :, :] - gram[2 * N : 2 * N + 8, :]
            )

            @pl.when(goes)
            def _():
                copy_AJ(i + 1, d + ahead).start()

            AL = dot(A, oL[i + 1], TN)
            B[...] = AL
            M[...] = dot(AL, A, NN)

        return ahead * 2

    lax.fori_loop(0, levels + 1, level, jnp.int32(1))

    g, z = gzs[0:1, :], gzs[2:3, :]
    S[:, 0:N] = oL[levels + 1] + jnp.where(eye, jnp.broadcast_to(g, (N, N)), 0.0)
    S[:, N : 2 * N] = unit
    S[:, 2 * N : 3 * N] = F.T
    factor((S.at[:, 0 : 3 * N], 3))
    K = S[:, 2 * N : 3 * N]
    pred = Q_ref[...] + dot(K, K, TN)
    K = S[:, N : 2 * N]
    cov = dot(K, K, TN)
    cov = 0.5 * (cov + cov.T)
    cov_ref[0] = cov
    mean = ob[levels + 1]
    mean = mean + dot(z - g * mean, cov, NN)
    mean_ref[0:1, :] = mean[0:1, :]
    g, z = gzs[1:2, :], gzs[3:4, :]
    across = jnp.broadcast_to(jnp.sqrt(g), (N, N))
    scaled = across.T * pred
    T[:, 0:N] = scaled * across + unit
    T[:, N:] = scaled
    factor((T, 2))
    K = T[:, N:]
    cov = pred - dot(K, K, TN)
    cov = 0.5 * (cov + cov.T)
    cov_ref[1] = cov
    mean = dot(mean, F, NT)
    mean = mean + dot(z - g * mean, cov, NN)
    mean_ref[1:2, :] = mean[0:1, :]

    @pl.when(d + 1 < devices)
    def _():
        gz_copy(d + 1).wait_send()

    def drain(i, ahead):
        @pl.when(d + ahead < devices)
        def _():
            copy_b(i + 1, d + ahead).wait_send()
            copy_L(i + 1, d + ahead).wait_send()

            @pl.when(d >= ahead)
            def _():
                copy_AJ(i + 1, d + ahead).wait_send()

        return ahead * 2

    lax.fori_loop(0, levels, drain, jnp.int32(1))


def local(outer, inner, obs, mask, smap, F, Q, r, pm, pv):
    devices = outer * inner
    levels = devices.bit_length() - 1
    vmem = pl.BlockSpec(memory_space=pltpu.VMEM)
    slots = levels + 2
    return pl.pallas_call(
        functools.partial(kernel, outer, inner),
        out_shape=(
            jax.ShapeDtypeStruct((2, N), F32),
            jax.ShapeDtypeStruct((2, N, N), F32),
        ),
        in_specs=[vmem] * 8,
        out_specs=(vmem, vmem),
        scratch_shapes=[
            pltpu.VMEM((slots, N, N), F32),
            pltpu.VMEM((slots, 8, N), F32),
            pltpu.VMEM((slots, 2 * N + 8, N), F32),
            pltpu.VMEM((slots, N, N), F32),
            pltpu.VMEM((slots, 8, N), F32),
            pltpu.VMEM((slots, 2 * N + 8, N), F32),
            pltpu.VMEM((N, N), F32),
            pltpu.VMEM((N, N), F32),
            pltpu.VMEM((N, 4 * N), F32),
            pltpu.VMEM((N, 2 * N), F32),
            pltpu.VMEM((8, N), F32),
            pltpu.VMEM((8, N), F32),
            pltpu.SemaphoreType.DMA((slots, 3)),
            pltpu.SemaphoreType.DMA((slots, 3)),
            pltpu.SemaphoreType.DMA((2,)),
        ],
        compiler_params=pltpu.CompilerParams(
            collective_id=0, has_side_effects=True, vmem_limit_bytes=48 * 1024 * 1024
        ),
    )(obs, mask, smap.reshape(1, N), F, Q, r.reshape(1, N), pm.reshape(1, N), pv.reshape(1, N))


def solution(mesh):
    outer, inner = mesh.shape["outer"], mesh.shape["inner"]
    split = P(("region", "outer", "inner"))
    return jax.shard_map(
        functools.partial(local, outer, inner),
        mesh=mesh,
        in_specs=(split, split, P("region"), P(), P(), P(), P("region"), P("region")),
        out_specs=(split, split),
        check_vma=False,
    )
```
